32 devices in a mesh: groups: 2 (over y), row: 4 (over z), col: 2 (over x), src: 2 (over core).
Axes of the slice: x: 2, y: 2, z: 4, core: 2. Of those that a mesh axis runs over, the one named last changes fastest.
Arguments:
- impedance: bfloat16 [1024, 49152], P(('groups', 'row'), ('col', 'src')), parts along dimension 0, may hold values from -0.0390625 to 0.0390625
- currents: bfloat16 [16, 49152], P('groups', ('col', 'src', 'row')), parts along dimension 0, may hold values from -6 to 6
- tested: bfloat16 [16, 512], P('groups', ('row', 'col', 'src')), parts along dimension 0, may hold values from -6 to 6
Outputs:
- forward_field: float32 [16, 512], P('groups', ('row', 'col', 'src')), parts along dimension 0
- adjoint_field: float32 [16, 49152], P('groups', ('col', 'src', 'row')), parts along dimension 0
The draws below stay inside these ranges and needn't reach their ends.
There are 2 independent parts, one for each index of `groups`. The reference program is written for one: setup_inputs(seed, part) draws one part's arguments, and reference() takes and returns one part's arrays. A program takes and returns all parts, laid end to end along the dimension named above; each array names one. Nothing has to cross between parts.
All inputs are finite; a program needn't handle non-finite values.
Results may differ from the reference program's by a relative error of at most 0.0003.
Values may be sent and summed in bfloat16 or wider, within the bound.
A program may use at most 64 MiB of HBM per device.

```python
import jax
import jax.numpy as jnp
from jax import lax

COLS = 49152
SRC = 8
ROWS = 512


def raised(array, stream_key, source, target, shards_of, factor):
    def block_of(position):
        return (jnp.arange(array.shape[position]) // (array.shape[position] // shards_of)).reshape((-1,) + (1,) * (array.ndim - 1 - position))

    near = jax.random.permutation(stream_key, shards_of)[block_of(target)]
    far = (block_of(target) + shards_of // 2) % shards_of
    return jnp.where((block_of(source) == near) | (block_of(source) == far), factor * array, array)


def block_levels(stream_key, shape, split, least, top_value):
    def one(position, blocks):
        heights = jax.random.uniform(jax.random.fold_in(jax.random.fold_in(stream_key, 6), position), (blocks,), jnp.float32, least / len(split), top_value / len(split))
        return jnp.repeat(jnp.exp(heights), shape[position] // blocks).reshape((-1,) + (1,) * (len(shape) - position - 1))

    factor_of = one(*split[0])
    for cut in split[1:]:
        factor_of = factor_of * one(*cut)
    return factor_of


def noise(rng, extent, scale, limit, pieces=(), dtype=jnp.bfloat16):
    drawn = jax.random.normal(rng, extent, jnp.float32) * scale
    if len(pieces) > 0:
        drawn = block_levels(rng, extent, pieces, -0.22, 0.18) * drawn
    return jnp.clip(drawn, min=-limit, max=limit).astype(dtype)


def bell_draw_with(own_key, shape, deviation, bound, shards, heavy, dtype=jnp.bfloat16):
    result = deviation * jax.random.normal(own_key, shape, jnp.float32)
    if shards:
        result = result * block_levels(own_key, shape, shards, -0.22, 0.18)
    return jnp.clip(raised(result, jax.random.fold_in(own_key, 3), *heavy), -bound, bound).astype(dtype)


def setup_inputs(seed: int = 0, part: int = 0) -> dict:
    arg_keys = jax.random.split(jax.random.key(seed), 4)
    part_splits = jax.random.split(jax.random.fold_in(arg_keys[3], part), 4)
    impedance = bell_draw_with(part_splits[0], (ROWS, COLS), COLS ** -0.5, 0.0390625, ((0, 4), (1, 4)), (0, 1, 4, 2.0))
    currents = noise(part_splits[1], (SRC, COLS), 1.0, 6.0, ((1, 16),))
    tested = noise(part_splits[2], (SRC, ROWS), 1.0, 6.0, ((1, 16),))
    return {"impedance": impedance, "currents": currents, "tested": tested}


def reference(impedance, currents, tested):
    forward_field = lax.dot_general(currents, impedance, (((1,), (1,)), ((), ())), preferred_element_type=jnp.float32)
    adjoint_field = jnp.dot(tested, impedance, preferred_element_type=jnp.float32)
    return forward_field, adjoint_field
```

```python
import functools

import jax
import jax.numpy as jnp
from jax import lax
from jax.experimental import pallas as pl
from jax.experimental.pallas import tpu as pltpu
from jax.sharding import PartitionSpec as P

MESH = pl.DeviceIdType.MESH
F32 = jnp.float32
BF16 = jnp.bfloat16


def plain(impedance, currents, tested):
    col_block = lax.all_gather(currents, "row", axis=1, tiled=True)
    row_block = lax.all_gather(tested, ("col", "src"), axis=1, tiled=True)
    forward_terms = lax.dot_general(
        col_block, impedance, (((1,), (1,)), ((), ())), preferred_element_type=F32
    )
    adjoint_terms = jnp.dot(row_block, impedance, preferred_element_type=F32)
    forward_field = lax.psum_scatter(forward_terms, ("col", "src"), scatter_dimension=1, tiled=True)
    adjoint_field = lax.psum_scatter(adjoint_terms, "row", scatter_dimension=1, tiled=True)
    return (forward_field, adjoint_field)


def kernel(
    n, nc, ns,
    imp_hbm, cur_ref, tes_ref, fwd_ref, adj_ref,
    imp, cur_all, tes_all, adj_out, adj_in, fwd_out, fwd_in,
    imp_sem, cur_send, cur_recv, tes_send, tes_recv, adj_send, adj_recv, fwd_send, fwd_recv,
):
    m = nc * ns
    s, width = cur_ref.shape
    rows = imp_hbm.shape[0]
    half = width // 2
    part = rows // m
    r = lax.axis_index("row")
    col, src = lax.axis_index("col"), lax.axis_index("src")
    q = col * ns + src

    def row_peer(k):
        return {"row": lax.rem(r + k, n)}

    def col_peer(k):
        p = lax.rem(q + k, m)
        return {"col": p // ns, "src": lax.rem(p, ns)}

    loads = []
    for k in range(n):
        first = pl.multiple_of(lax.rem(r + k, n) * width, width)
        copy = pltpu.make_async_copy(imp_hbm.at[:, pl.ds(first, width)], imp.at[k], imp_sem.at[k])
        copy.start()
        loads.append(copy)

    barrier = pltpu.get_barrier_semaphore()
    for k in range(1, n):
        pl.semaphore_signal(barrier, inc=1, device_id=row_peer(k), device_id_type=MESH)
    for k in range(1, m):
        pl.semaphore_signal(barrier, inc=1, device_id=col_peer(k), device_id_type=MESH)

    lane = lax.broadcasted_iota(jnp.int32, (s, rows), 1)
    spread = jnp.concatenate([tes_ref[...].astype(F32)] * m, axis=1)
    tes_all[0] = jnp.where(lane // part == q, spread, 0.0)
    cur = cur_ref[...].astype(F32)
    cur_all[0] = jnp.concatenate([cur[:, :half], cur[:, half:]], axis=0).astype(BF16)

    pl.semaphore_wait(barrier, n - 1 + m - 1)

    def push(ref_out, ref_in, send, recv, k, peer):
        copy = pltpu.make_async_remote_copy(
            src_ref=ref_out, dst_ref=ref_in, send_sem=send.at[k], recv_sem=recv.at[k],
            device_id=peer, device_id_type=MESH,
        )
        copy.start()
        return copy

    tes_copies = [push(tes_all.at[0], tes_all.at[m - k], tes_send, tes_recv, k, col_peer(k)) for k in range(1, m)]
    cur_copies = [push(cur_all.at[0], cur_all.at[n - k], cur_send, cur_recv, k, row_peer(k)) for k in range(1, n)]

    def forward_terms(k):
        both = cur_all[k]
        dims = (((1,), (1,)), ((), ()))
        low = lax.dot_general(both, imp[k, :, :half], dims, preferred_element_type=F32)
        high = lax.dot_general(both, imp[k, :, half:], dims, preferred_element_type=F32)
        return low[:s] + high[s:]

    for copy in tes_copies:
        copy.wait_recv()
    row_block = tes_all[0]
    for k in range(1, m):
        row_block = row_block + tes_all[k]
    row_block = row_block.astype(BF16)

    adj_copies = []
    for k in list(range(1, n)) + [0]:
        loads[k].wait()
        adj_out[k] = jnp.dot(row_block, imp[k], preferred_element_type=F32)
        if k:
            adj_copies.append(push(adj_out.at[k], adj_in.at[n - k], adj_send, adj_recv, k, row_peer(k)))

    total = forward_terms(0)
    for k in range(1, n):
        cur_copies[n - k - 1].wait_recv()
        total = total + forward_terms(k)
    fwd_out[...] = total
    fwd_copies = [push(fwd_out, fwd_in.at[m - k], fwd_send, fwd_recv, k, col_peer(k)) for k in range(1, m)]

    result = adj_out[0]
    for copy, k in zip(adj_copies, range(1, n)):
        copy.wait_recv()
        result = result + adj_in[n - k]
    adj_ref[...] = result

    for copy, k in zip(fwd_copies, range(1, m)):
        copy.wait_recv()
        total = total + fwd_in[m - k]
    mine = total[:, :part]
    for k in range(1, m):
        mine = jnp.where(q == k, total[:, k * part : (k + 1) * part], mine)
    fwd_ref[...] = mine

    for copy in tes_copies + cur_copies + adj_copies + fwd_copies:
        copy.wait_send()


def fused(n, nc, ns, impedance, currents, tested):
    m = nc * ns
    rows, _ = impedance.shape
    s, width = currents.shape
    part = rows // m
    vmem = pl.BlockSpec(memory_space=pltpu.VMEM)
    dma = pltpu.SemaphoreType.DMA
    return pl.pallas_call(
        functools.partial(kernel, n, nc, ns),
        out_shape=(
            jax.ShapeDtypeStruct((s, part), F32),
            jax.ShapeDtypeStruct((s, width), F32),
        ),
        in_specs=[pl.BlockSpec(memory_space=pl.ANY), vmem, vmem],
        out_specs=(vmem, vmem),
        scratch_shapes=[
            pltpu.VMEM((n, rows, width), BF16),
            pltpu.VMEM((n, 2 * s, width // 2), BF16),
            pltpu.VMEM((m, s, rows), F32),
            pltpu.VMEM((n, s, width), F32),
            pltpu.VMEM((n, s, width), F32),
            pltpu.VMEM((s, rows), F32),
            pltpu.VMEM((m, s, rows), F32),
            dma((n,)), dma((n,)), dma((n,)), dma((m,)), dma((m,)),
            dma((n,)), dma((n,)), dma((m,)), dma((m,)),
        ],
        compiler_params=pltpu.CompilerParams(
            collective_id=0, has_side_effects=True, vmem_limit_bytes=32 * 1024 * 1024
        ),
        cost_estimate=pl.CostEstimate(
            flops=4 * s * rows * width * n, bytes_accessed=2 * rows * width * n, transcendentals=0
        ),
    )(impedance, currents, tested)


def solution(mesh):
    n, nc, ns = mesh.shape["row"], mesh.shape["col"], mesh.shape["src"]

    def body(impedance, currents, tested):
        s, width = currents.shape
        rows = impedance.shape[0]
        if s == 8 and width % 256 == 0 and rows % 128 == 0:
            return fused(n, nc, ns, impedance, currents, tested)
        return plain(impedance, currents, tested)

    placed = (
        P(("groups", "row"), ("col", "src")),
        P("groups", ("col", "src", "row")),
        P("groups", ("row", "col", "src")),
    )
    return jax.shard_map(
        body,
        mesh=mesh,
        in_specs=placed,
        out_specs=(P("groups", ("row", "col", "src")), P("groups", ("col", "src", "row"))),
        check_vma=False,
    )
```

```python
import functools

import jax
import jax.numpy as jnp
from jax import lax
from jax.experimental import pallas as pl
from jax.experimental.pallas import tpu as pltpu
from jax.sharding import PartitionSpec as P

MESH = pl.DeviceIdType.MESH
F32 = jnp.float32
BF16 = jnp.bfloat16
SPAN = 2.0**14


def plain(impedance, currents, tested):
    col_block = lax.all_gather(currents, "row", axis=1, tiled=True)
    row_block = lax.all_gather(tested, ("col", "src"), axis=1, tiled=True)
    forward_terms = lax.dot_general(
        col_block, impedance, (((1,), (1,)), ((), ())), preferred_element_type=F32
    )
    adjoint_terms = jnp.dot(row_block, impedance, preferred_element_type=F32)
    forward_field = lax.psum_scatter(forward_terms, ("col", "src"), scatter_dimension=1, tiled=True)
    adjoint_field = lax.psum_scatter(adjoint_terms, "row", scatter_dimension=1, tiled=True)
    return (forward_field, adjoint_field)


def encode(block):
    s, width = block.shape
    half = width // 2
    top = jnp.max(jnp.abs(block), axis=1, keepdims=True).astype(BF16).astype(F32)
    scale = jnp.where(top > 0.0, 1.0 / top, 0.0)
    unit = block * scale * SPAN
    square = unit * unit
    fourth = square * square
    eighth = fourth * fourth
    coded = jnp.where(unit < 0.0, -eighth, eighth)
    tops = jnp.broadcast_to(top, (s, 128))
    low = jnp.concatenate([coded[:, :half], tops], axis=1)
    high = jnp.concatenate([coded[:, half:], tops], axis=1)
    return jnp.concatenate([low, high], axis=0).astype(BF16)


def decode(wire):
    both, cols = wire.shape
    s, half = both // 2, cols - 128
    coded = wire.astype(F32)
    coded = jnp.concatenate([coded[:s, :half], coded[s:, :half]], axis=1)
    top = wire.astype(F32)[:s, half : half + 1] * (1.0 / SPAN)
    size = jnp.abs(coded)
    fourth_root = lax.rsqrt(lax.rsqrt(size))
    root = fourth_root * lax.rsqrt(fourth_root)
    root = jnp.where(size > 0.0, root, 0.0) * top
    return jnp.where(coded < 0.0, -root, root)


def kernel(
    n, nc, ns,
    imp_hbm, cur_hbm, tes_hbm, fwd_ref, adj_ref,
    imp, cur_ref, cur_all, tes_all, adj_out, adj_in, fwd_out, fwd_in,
    in_sem, imp_sem, cur_send, cur_recv, tes_send, tes_recv, adj_send, adj_recv, fwd_send, fwd_recv,
):
    m = nc * ns
    s, width = cur_hbm.shape
    rows = imp_hbm.shape[0]
    part = rows // m
    r = lax.axis_index("row")
    q = lax.axis_index("col") * ns + lax.axis_index("src")

    def row_at(k):
        return lax.rem(r + k, n)

    def row_peer(k):
        return {"row": row_at(k)}

    def col_peer(k):
        p = lax.rem(q + k, m)
        return {"col": p // ns, "src": lax.rem(p, ns)}

    tes_load = pltpu.make_async_copy(tes_hbm, tes_all.at[q], in_sem.at[0])
    tes_load.start()
    cur_load = pltpu.make_async_copy(cur_hbm, cur_ref, in_sem.at[1])
    cur_load.start()
    loads = []
    for k in range(n):
        first = pl.multiple_of(row_at(k) * width, width)
        copy = pltpu.make_async_copy(imp_hbm.at[:, pl.ds(first, width)], imp.at[k], imp_sem.at[k])
        copy.start()
        loads.append(copy)

    barrier = pltpu.get_barrier_semaphore()
    for k in range(1, m):
        pl.semaphore_signal(barrier, inc=1, device_id=col_peer(k), device_id_type=MESH)
    for k in range(1, n):
        pl.semaphore_signal(barrier, inc=1, device_id=row_peer(k), device_id_type=MESH)

    cur_load.wait()
    half = width // 2
    cur = cur_ref[...].astype(F32)
    cur_all[0] = jnp.concatenate([cur[:, :half], cur[:, half:]], axis=0).astype(BF16)
    tes_load.wait()
    pl.semaphore_wait(barrier, n - 1 + m - 1)

    def push(ref_out, ref_in, send, recv, k, peer):
        copy = pltpu.make_async_remote_copy(
            src_ref=ref_out, dst_ref=ref_in, send_sem=send.at[k], recv_sem=recv.at[k],
            device_id=peer, device_id_type=MESH,
        )
        copy.start()
        return copy

    away = list(range(1, n))
    tes_copies = [push(tes_all.at[q], tes_all.at[q], tes_send, tes_recv, k, col_peer(k)) for k in range(1, m)]
    cur_copies = [push(cur_all.at[0], cur_all.at[n - k], cur_send, cur_recv, k, row_peer(k)) for k in away]

    def forward_terms(k):
        both = cur_all[k]
        dims = (((1,), (1,)), ((), ()))
        low = lax.dot_general(both, imp[k, :, :half], dims, preferred_element_type=F32)
        high = lax.dot_general(both, imp[k, :, half:], dims, preferred_element_type=F32)
        return low[:s] + high[s:]

    for copy in tes_copies:
        copy.wait_recv()
    row_block = jnp.concatenate([tes_all[p].astype(F32) for p in range(m)], axis=1).astype(BF16)

    adj_copies = []
    for k in away:
        loads[k].wait()
        adj_out[k] = encode(jnp.dot(row_block, imp[k], preferred_element_type=F32))
        adj_copies.append(push(adj_out.at[k], adj_in.at[n - k], adj_send, adj_recv, k, row_peer(k)))

    loads[0].wait()
    total = forward_terms(0)
    for copy, k in zip(cur_copies, away):
        copy.wait_recv()
        total = total + forward_terms(n - k)
    fwd_out[...] = total
    fwd_copies = [push(fwd_out, fwd_in.at[m - k], fwd_send, fwd_recv, k, col_peer(k)) for k in range(1, m)]

    result = jnp.dot(row_block, imp[0], preferred_element_type=F32)
    for copy, k in zip(reversed(adj_copies), reversed(away)):
        copy.wait_recv()
        result = result + decode(adj_in[n - k])
    adj_ref[...] = result

    for copy, k in zip(fwd_copies, range(1, m)):
        copy.wait_recv()
        total = total + fwd_in[m - k]
    mine = total[:, :part]
    for k in range(1, m):
        mine = jnp.where(q == k, total[:, k * part : (k + 1) * part], mine)
    fwd_ref[...] = mine

    for copy in tes_copies + cur_copies + adj_copies + fwd_copies:
        copy.wait_send()


def fused(n, nc, ns, impedance, currents, tested):
    m = nc * ns
    rows, _ = impedance.shape
    s, width = currents.shape
    part = rows // m
    vmem = pl.BlockSpec(memory_space=pltpu.VMEM)
    dma = pltpu.SemaphoreType.DMA
    return pl.pallas_call(
        functools.partial(kernel, n, nc, ns),
        out_shape=(pltpu.VMEM((s, part), F32), pltpu.VMEM((s, width), F32)),
        in_specs=[pl.BlockSpec(memory_space=pltpu.HBM)] * 3,
        out_specs=(vmem, vmem),
        scratch_shapes=[
            pltpu.VMEM((n, rows, width), BF16),
            pltpu.VMEM((s, width), BF16),
            pltpu.VMEM((n, 2 * s, width // 2), BF16),
            pltpu.VMEM((m, s, part), BF16),
            pltpu.VMEM((n, 2 * s, width // 2 + 128), BF16),
            pltpu.VMEM((n, 2 * s, width // 2 + 128), BF16),
            pltpu.VMEM((s, rows), F32),
            pltpu.VMEM((m, s, rows), F32),
            dma((2,)), dma((n,)), dma((n,)), dma((n,)), dma((m,)), dma((m,)),
            dma((n,)), dma((n,)), dma((m,)), dma((m,)),
        ],
        compiler_params=pltpu.CompilerParams(
            collective_id=0, has_side_effects=True, vmem_limit_bytes=32 * 1024 * 1024
        ),
        cost_estimate=pl.CostEstimate(
            flops=4 * s * rows * width * n, bytes_accessed=2 * rows * width * n, transcendentals=0
        ),
    )(*[pltpu.with_memory_space_constraint(x, pltpu.HBM) for x in (impedance, currents, tested)])


def solution(mesh):
    n, nc, ns = mesh.shape["row"], mesh.shape["col"], mesh.shape["src"]

    def body(impedance, currents, tested):
        s, width = currents.shape
        rows = impedance.shape[0]
        if s == 8 and n & (n - 1) == 0 and width % 256 == 0 and rows % 128 == 0:
            return fused(n, nc, ns, impedance, currents, tested)
        return plain(impedance, currents, tested)

    placed = (
        P(("groups", "row"), ("col", "src")),
        P("groups", ("col", "src", "row")),
        P("groups", ("row", "col", "src")),
    )
    return jax.shard_map(
        body,
        mesh=mesh,
        in_specs=placed,
        out_specs=(P("groups", ("row", "col", "src")), P("groups", ("col", "src", "row"))),
        check_vma=False,
    )
```

```python
import functools

import jax
import jax.numpy as jnp
from jax import lax
from jax.experimental import pallas as pl
from jax.experimental.pallas import tpu as pltpu
from jax.sharding import PartitionSpec as P

MESH = pl.DeviceIdType.MESH
F32 = jnp.float32
BF16 = jnp.bfloat16
SPAN = 2.0**14


def plain(impedance, currents, tested):
    col_block = lax.all_gather(currents, "row", axis=1, tiled=True)
    row_block = lax.all_gather(tested, ("col", "src"), axis=1, tiled=True)
    forward_terms = lax.dot_general(
        col_block, impedance, (((1,), (1,)), ((), ())), preferred_element_type=F32
    )
    adjoint_terms = jnp.dot(row_block, impedance, preferred_element_type=F32)
    forward_field = lax.psum_scatter(forward_terms, ("col", "src"), scatter_dimension=1, tiled=True)
    adjoint_field = lax.psum_scatter(adjoint_terms, "row", scatter_dimension=1, tiled=True)
    return (forward_field, adjoint_field)


def encode(block):
    s, width = block.shape
    half = width // 2
    top = jnp.max(jnp.abs(block), axis=1, keepdims=True).astype(BF16).astype(F32)
    scale = jnp.where(top > 0.0, 1.0 / top, 0.0)
    unit = block * scale * SPAN
    square = unit * unit
    fourth = square * square
    eighth = fourth * fourth
    coded = jnp.where(unit < 0.0, -eighth, eighth)
    tops = jnp.broadcast_to(top, (s, 128))
    low = jnp.concatenate([coded[:, :half], tops], axis=1)
    high = jnp.concatenate([coded[:, half:], tops], axis=1)
    return jnp.concatenate([low, high], axis=0).astype(BF16)


def decode(wire):
    both, cols = wire.shape
    s, half = both // 2, cols - 128
    coded = wire.astype(F32)
    coded = jnp.concatenate([coded[:s, :half], coded[s:, :half]], axis=1)
    top = wire.astype(F32)[:s, half : half + 1] * (1.0 / SPAN)
    size = jnp.abs(coded)
    fourth_root = lax.rsqrt(lax.rsqrt(size))
    root = fourth_root * lax.rsqrt(fourth_root)
    root = jnp.where(size > 0.0, root, 0.0) * top
    return jnp.where(coded < 0.0, -root, root)


def kernel(
    n, nc, ns,
    imp_hbm, cur_hbm, tes_hbm, fwd_ref, adj_ref,
    imp, cur_ref, cur_all, tes_all, adj_out, adj_in, fwd_out, fwd_in,
    in_sem, imp_sem, cur_send, cur_recv, tes_send, tes_recv, adj_send, adj_recv, fwd_send, fwd_recv,
):
    m = nc * ns
    s, width = cur_hbm.shape
    rows = imp_hbm.shape[0]
    part = rows // m
    r = lax.axis_index("row")
    q = lax.axis_index("col") * ns + lax.axis_index("src")

    def row_at(k):
        return lax.rem(r + k, n)

    def row_peer(k):
        return {"row": row_at(k)}

    def col_peer(k):
        p = lax.rem(q + k, m)
        return {"col": p // ns, "src": lax.rem(p, ns)}

    tes_load = pltpu.make_async_copy(tes_hbm, tes_all.at[q], in_sem.at[0])
    tes_load.start()
    cur_load = pltpu.make_async_copy(cur_hbm, cur_ref, in_sem.at[1])
    cur_load.start()
    barrier = pltpu.get_barrier_semaphore()
    for k in range(1, m):
        pl.semaphore_signal(barrier, inc=1, device_id=col_peer(k), device_id_type=MESH)
    for k in range(1, n):
        pl.semaphore_signal(barrier, inc=1, device_id=row_peer(k), device_id_type=MESH)

    loads = []
    for k in range(n):
        first = pl.multiple_of(row_at(k) * width, width)
        copy = pltpu.make_async_copy(imp_hbm.at[:, pl.ds(first, width)], imp.at[k], imp_sem.at[k])
        copy.start()
        loads.append(copy)

    cur_load.wait()
    half = width // 2
    cur = cur_ref[...].astype(F32)
    cur_all[0] = jnp.concatenate([cur[:, :half], cur[:, half:]], axis=0).astype(BF16)
    tes_load.wait()
    pl.semaphore_wait(barrier, n - 1 + m - 1)

    def push(ref_out, ref_in, send, recv, k, peer):
        copy = pltpu.make_async_remote_copy(
            src_ref=ref_out, dst_ref=ref_in, send_sem=send.at[k], recv_sem=recv.at[k],
            device_id=peer, device_id_type=MESH,
        )
        copy.start()
        return copy

    away = list(range(1, n))
    tes_copies = [push(tes_all.at[q], tes_all.at[q], tes_send, tes_recv, k, col_peer(k)) for k in range(1, m)]
    cur_copies = [push(cur_all.at[0], cur_all.at[n - k], cur_send, cur_recv, k, row_peer(k)) for k in away]

    def forward_terms(k):
        both = cur_all[k]
        dims = (((1,), (1,)), ((), ()))
        low = lax.dot_general(both, imp[k, :, :half], dims, preferred_element_type=F32)
        high = lax.dot_general(both, imp[k, :, half:], dims, preferred_element_type=F32)
        return low[:s] + high[s:]

    for copy in tes_copies:
        copy.wait_recv()
    row_block = jnp.concatenate([tes_all[p].astype(F32) for p in range(m)], axis=1).astype(BF16)

    adj_copies = []
    for k in away:
        loads[k].wait()
        adj_out[k] = encode(jnp.dot(row_block, imp[k], preferred_element_type=F32))
        adj_copies.append(push(adj_out.at[k], adj_in.at[n - k], adj_send, adj_recv, k, row_peer(k)))

    loads[0].wait()
    total = forward_terms(0)
    for copy, k in zip(cur_copies, away):
        copy.wait_recv()
        total = total + forward_terms(n - k)
    fwd_out[...] = total
    fwd_copies = [push(fwd_out, fwd_in.at[m - k], fwd_send, fwd_recv, k, col_peer(k)) for k in range(1, m)]

    result = jnp.dot(row_block, imp[0], preferred_element_type=F32)
    for copy, k in zip(adj_copies, away):
        copy.wait_recv()
        result = result + decode(adj_in[n - k])
    adj_ref[...] = result

    for copy, k in zip(fwd_copies, range(1, m)):
        copy.wait_recv()
        total = total + fwd_in[m - k]
    mine = total[:, :part]
    for k in range(1, m):
        mine = jnp.where(q == k, total[:, k * part : (k + 1) * part], mine)
    fwd_ref[...] = mine

    for copy in tes_copies + cur_copies + adj_copies + fwd_copies:
        copy.wait_send()


def deliver(fwd_ref, adj_ref, fwd_hbm, adj_hbm, sem):
    adj_copy = pltpu.make_async_copy(adj_ref, adj_hbm, sem.at[0])
    fwd_copy = pltpu.make_async_copy(fwd_ref, fwd_hbm, sem.at[1])
    adj_copy.start()
    fwd_copy.start()
    adj_copy.wait()
    fwd_copy.wait()


def fused(n, nc, ns, impedance, currents, tested):
    m = nc * ns
    rows, _ = impedance.shape
    s, width = currents.shape
    part = rows // m
    vmem = pl.BlockSpec(memory_space=pltpu.VMEM)
    dma = pltpu.SemaphoreType.DMA
    fields = pl.pallas_call(
        functools.partial(kernel, n, nc, ns),
        out_shape=(pltpu.VMEM((s, part), F32), pltpu.VMEM((s, width), F32)),
        in_specs=[pl.BlockSpec(memory_space=pltpu.HBM)] * 3,
        out_specs=(vmem, vmem),
        scratch_shapes=[
            pltpu.VMEM((n, rows, width), BF16),
            pltpu.VMEM((s, width), BF16),
            pltpu.VMEM((n, 2 * s, width // 2), BF16),
            pltpu.VMEM((m, s, part), BF16),
            pltpu.VMEM((n, 2 * s, width // 2 + 128), BF16),
            pltpu.VMEM((n, 2 * s, width // 2 + 128), BF16),
            pltpu.VMEM((s, rows), F32),
            pltpu.VMEM((m, s, rows), F32),
            dma((2,)), dma((n,)), dma((n,)), dma((n,)), dma((m,)), dma((m,)),
            dma((n,)), dma((n,)), dma((m,)), dma((m,)),
        ],
        compiler_params=pltpu.CompilerParams(
            collective_id=0, has_side_effects=True, vmem_limit_bytes=32 * 1024 * 1024
        ),
        cost_estimate=pl.CostEstimate(
            flops=4 * s * rows * width * n, bytes_accessed=2 * rows * width * n, transcendentals=0
        ),
    )(*[pltpu.with_memory_space_constraint(x, pltpu.HBM) for x in (impedance, currents, tested)])
    return pl.pallas_call(
        deliver,
        out_shape=(pltpu.HBM((s, part), F32), pltpu.HBM((s, width), F32)),
        in_specs=[vmem, vmem],
        out_specs=(pl.BlockSpec(memory_space=pltpu.HBM), pl.BlockSpec(memory_space=pltpu.HBM)),
        scratch_shapes=[dma((2,))],
    )(*[pltpu.with_memory_space_constraint(x, pltpu.VMEM) for x in fields])


def solution(mesh):
    n, nc, ns = mesh.shape["row"], mesh.shape["col"], mesh.shape["src"]

    def body(impedance, currents, tested):
        s, width = currents.shape
        rows = impedance.shape[0]
        if s == 8 and n & (n - 1) == 0 and width % 256 == 0 and rows % 128 == 0:
            return fused(n, nc, ns, impedance, currents, tested)
        return plain(impedance, currents, tested)

    placed = (
        P(("groups", "row"), ("col", "src")),
        P("groups", ("col", "src", "row")),
        P("groups", ("row", "col", "src")),
    )
    return jax.shard_map(
        body,
        mesh=mesh,
        in_specs=placed,
        out_specs=(P("groups", ("row", "col", "src")), P("groups", ("col", "src", "row"))),
        check_vma=False,
    )
```

```python
import functools

import jax
import jax.numpy as jnp
from jax import lax
from jax.experimental import pallas as pl
from jax.experimental.pallas import tpu as pltpu
from jax.sharding import PartitionSpec as P

MESH = pl.DeviceIdType.MESH
F32 = jnp.float32
BF16 = jnp.bfloat16
SPAN = 2.0**14


def plain(impedance, currents, tested):
    col_block = lax.all_gather(currents, "row", axis=1, tiled=True)
    row_block = lax.all_gather(tested, ("col", "src"), axis=1, tiled=True)
    forward_terms = lax.dot_general(
        col_block, impedance, (((1,), (1,)), ((), ())), preferred_element_type=F32
    )
    adjoint_terms = jnp.dot(row_block, impedance, preferred_element_type=F32)
    forward_field = lax.psum_scatter(forward_terms, ("col", "src"), scatter_dimension=1, tiled=True)
    adjoint_field = lax.psum_scatter(adjoint_terms, "row", scatter_dimension=1, tiled=True)
    return (forward_field, adjoint_field)


def encode(block):
    s, width = block.shape
    half = width // 2
    top = jnp.max(jnp.abs(block), axis=1, keepdims=True).astype(BF16).astype(F32)
    scale = jnp.where(top > 0.0, 1.0 / top, 0.0)
    unit = block * scale * SPAN
    square = unit * unit
    fourth = square * square
    eighth = fourth * fourth
    coded = jnp.where(unit < 0.0, -eighth, eighth)
    tops = jnp.broadcast_to(top, (s, 128))
    low = jnp.concatenate([coded[:, :half], tops], axis=1)
    high = jnp.concatenate([coded[:, half:], tops], axis=1)
    return jnp.concatenate([low, high], axis=0).astype(BF16)


def decode(wire):
    both, cols = wire.shape
    s, half = both // 2, cols - 128
    coded = wire.astype(F32)
    coded = jnp.concatenate([coded[:s, :half], coded[s:, :half]], axis=1)
    top = wire.astype(F32)[:s, half : half + 1] * (1.0 / SPAN)
    size = jnp.abs(coded)
    fourth_root = lax.rsqrt(lax.rsqrt(size))
    root = fourth_root * lax.rsqrt(fourth_root)
    root = jnp.where(size > 0.0, root, 0.0) * top
    return jnp.where(coded < 0.0, -root, root)


def kernel(
    n, nc, ns,
    imp_hbm, cur_hbm, tes_hbm, fwd_ref, adj_ref,
    imp, cur_ref, cur_all, tes_all, adj_out, adj_in, fwd_out, fwd_in,
    in_sem, imp_sem, cur_send, cur_recv, tes_send, tes_recv, adj_send, adj_recv, fwd_send, fwd_recv,
):
    m = nc * ns
    s, width = cur_hbm.shape
    rows = imp_hbm.shape[0]
    part = rows // m
    r = lax.axis_index("row")
    q = lax.axis_index("col") * ns + lax.axis_index("src")

    def row_at(k):
        return lax.rem(r + k, n)

    def row_peer(k):
        return {"row": row_at(k)}

    def col_peer(k):
        p = lax.rem(q + k, m)
        return {"col": p // ns, "src": lax.rem(p, ns)}

    tes_load = pltpu.make_async_copy(tes_hbm, tes_all.at[q], in_sem.at[0])
    tes_load.start()
    cur_load = pltpu.make_async_copy(cur_hbm, cur_ref, in_sem.at[1])
    cur_load.start()
    barrier = pltpu.get_barrier_semaphore()
    for k in range(1, m):
        pl.semaphore_signal(barrier, inc=1, device_id=col_peer(k), device_id_type=MESH)
    for k in range(1, n):
        pl.semaphore_signal(barrier, inc=1, device_id=row_peer(k), device_id_type=MESH)

    loads = [None] * n
    for k in list(range(1, n)) + [0]:
        first = pl.multiple_of(row_at(k) * width, width)
        copy = pltpu.make_async_copy(imp_hbm.at[:, pl.ds(first, width)], imp.at[k], imp_sem.at[k])
        copy.start()
        loads[k] = copy

    cur_load.wait()
    half = width // 2
    cur = cur_ref[...].astype(F32)
    cur_all[0] = jnp.concatenate([cur[:, :half], cur[:, half:]], axis=0).astype(BF16)
    tes_load.wait()
    pl.semaphore_wait(barrier, n - 1 + m - 1)

    def push(ref_out, ref_in, send, recv, k, peer):
        copy = pltpu.make_async_remote_copy(
            src_ref=ref_out, dst_ref=ref_in, send_sem=send.at[k], recv_sem=recv.at[k],
            device_id=peer, device_id_type=MESH,
        )
        copy.start()
        return copy

    away = list(range(1, n))
    tes_copies = [push(tes_all.at[q], tes_all.at[q], tes_send, tes_recv, k, col_peer(k)) for k in range(1, m)]
    cur_copies = [push(cur_all.at[0], cur_all.at[n - k], cur_send, cur_recv, k, row_peer(k)) for k in away]

    def forward_terms(k):
        both = cur_all[k]
        dims = (((1,), (1,)), ((), ()))
        low = lax.dot_general(both, imp[k, :, :half], dims, preferred_element_type=F32)
        high = lax.dot_general(both, imp[k, :, half:], dims, preferred_element_type=F32)
        return low[:s] + high[s:]

    for copy in tes_copies:
        copy.wait_recv()
    row_block = jnp.concatenate([tes_all[p].astype(F32) for p in range(m)], axis=1).astype(BF16)

    adj_copies = []
    for k in away:
        loads[k].wait()
        adj_out[k] = encode(jnp.dot(row_block, imp[k], preferred_element_type=F32))
        adj_copies.append(push(adj_out.at[k], adj_in.at[n - k], adj_send, adj_recv, k, row_peer(k)))

    loads[0].wait()
    total = forward_terms(0)
    for copy, k in zip(cur_copies, away):
        copy.wait_recv()
        total = total + forward_terms(n - k)
    fwd_out[...] = total
    fwd_copies = [push(fwd_out, fwd_in.at[m - k], fwd_send, fwd_recv, k, col_peer(k)) for k in range(1, m)]

    result = jnp.dot(row_block, imp[0], preferred_element_type=F32)
    for copy, k in zip(adj_copies, away):
        copy.wait_recv()
        result = result + decode(adj_in[n - k])
    adj_ref[...] = result

    for copy, k in zip(fwd_copies, range(1, m)):
        copy.wait_recv()
        total = total + fwd_in[m - k]
    mine = total[:, :part]
    for k in range(1, m):
        mine = jnp.where(q == k, total[:, k * part : (k + 1) * part], mine)
    fwd_ref[...] = mine

    for copy in tes_copies + cur_copies + adj_copies + fwd_copies:
        copy.wait_send()


def deliver(fwd_ref, adj_ref, fwd_hbm, adj_hbm, sem):
    adj_copy = pltpu.make_async_copy(adj_ref, adj_hbm, sem.at[0])
    fwd_copy = pltpu.make_async_copy(fwd_ref, fwd_hbm, sem.at[1])
    adj_copy.start()
    fwd_copy.start()
    adj_copy.wait()
    fwd_copy.wait()


def fused(n, nc, ns, impedance, currents, tested):
    m = nc * ns
    rows, _ = impedance.shape
    s, width = currents.shape
    part = rows // m
    vmem = pl.BlockSpec(memory_space=pltpu.VMEM)
    dma = pltpu.SemaphoreType.DMA
    fields = pl.pallas_call(
        functools.partial(kernel, n, nc, ns),
        out_shape=(pltpu.VMEM((s, part), F32), pltpu.VMEM((s, width), F32)),
        in_specs=[pl.BlockSpec(memory_space=pltpu.HBM)] * 3,
        out_specs=(vmem, vmem),
        scratch_shapes=[
            pltpu.VMEM((n, rows, width), BF16),
            pltpu.VMEM((s, width), BF16),
            pltpu.VMEM((n, 2 * s, width // 2), BF16),
            pltpu.VMEM((m, s, part), BF16),
            pltpu.VMEM((n, 2 * s, width // 2 + 128), BF16),
            pltpu.VMEM((n, 2 * s, width // 2 + 128), BF16),
            pltpu.VMEM((s, rows), F32),
            pltpu.VMEM((m, s, rows), F32),
            dma((2,)), dma((n,)), dma((n,)), dma((n,)), dma((m,)), dma((m,)),
            dma((n,)), dma((n,)), dma((m,)), dma((m,)),
        ],
        compiler_params=pltpu.CompilerParams(
            collective_id=0, has_side_effects=True, vmem_limit_bytes=32 * 1024 * 1024
        ),
        cost_estimate=pl.CostEstimate(
            flops=4 * s * rows * width * n, bytes_accessed=2 * rows * width * n, transcendentals=0
        ),
    )(*[pltpu.with_memory_space_constraint(x, pltpu.HBM) for x in (impedance, currents, tested)])
    return pl.pallas_call(
        deliver,
        out_shape=(pltpu.HBM((s, part), F32), pltpu.HBM((s, width), F32)),
        in_specs=[vmem, vmem],
        out_specs=(pl.BlockSpec(memory_space=pltpu.HBM), pl.BlockSpec(memory_space=pltpu.HBM)),
        scratch_shapes=[dma((2,))],
    )(*[pltpu.with_memory_space_constraint(x, pltpu.VMEM) for x in fields])


def solution(mesh):
    n, nc, ns = mesh.shape["row"], mesh.shape["col"], mesh.shape["src"]

    def body(impedance, currents, tested):
        s, width = currents.shape
        rows = impedance.shape[0]
        if s == 8 and n & (n - 1) == 0 and width % 256 == 0 and rows % 128 == 0:
            return fused(n, nc, ns, impedance, currents, tested)
        return plain(impedance, currents, tested)

    placed = (
        P(("groups", "row"), ("col", "src")),
        P("groups", ("col", "src", "row")),
        P("groups", ("row", "col", "src")),
    )
    return jax.shard_map(
        body,
        mesh=mesh,
        in_specs=placed,
        out_specs=(P("groups", ("row", "col", "src")), P("groups", ("col", "src", "row"))),
        check_vma=False,
    )
```
